32 devices in a mesh: ctx: 16 (over z, y, core), head: 2 (over x).
Axes of the slice: x: 2, y: 2, z: 4, core: 2. Of those that a mesh axis runs over, the one named last changes fastest.
Arguments:
- queries: bfloat16 [768, 8192], P('ctx', 'head'), may hold values from -120 to 120
- cached_keys: bfloat16 [5120, 1024], P('ctx', 'head'), may hold values from -5 to 15
- cached_values: bfloat16 [5120, 1024], P('ctx', 'head'), may hold values from -6 to 6
- fresh_keys: bfloat16 [768, 1024], P('ctx', 'head'), may hold values from -5 to 15
- fresh_values: bfloat16 [768, 1024], P('ctx', 'head'), may hold values from -6 to 6
- recompute_index: int32 [16, 48], P('ctx'), may hold values from 0 to 319, as said below
- recompute_count: int32 [16], P('ctx'), may hold values from 1 to 48, 672 in all
- group_offsets: int32 [16], replicated, may hold values from 0 to 9585, as said below
Outputs:
- attention: bfloat16 [768, 8192], P('ctx', 'head')
- joined_keys: bfloat16 [5120, 1024], P('ctx', 'head')
- joined_values: bfloat16 [5120, 1024], P('ctx', 'head')
- drift: float32 [16, 48], P('ctx')
The draws below stay inside these ranges and needn't reach their ends.
Inputs may be any that keep to these rules, and one draw needn't show every extreme that they name: `recompute_index`: the entries of one group's row are different token numbers of that group. group_offsets[c + 1] - group_offsets[c] lies between 320 and 639.
All inputs are finite; a program needn't handle non-finite values. No bound on the sum of `recompute_count` on one device may be relied on, other than what follows from the above.
Results may differ from the reference program's by a relative error of at most 0.008.
Values may be sent and summed in bfloat16 or wider, within the bound.
A program may use at most 64 MiB of HBM per device.

```python
import math
import jax
import jax.numpy as jnp
import numpy as np
from jax import lax

HEADS = 64
KV_HEADS = 8
HEAD_DIM = 128
GROUP_LEN = 320
R_MAX = 48
GROUPS = 16
TOKENS = 5120
ROWS = 768


def key_draw(key, row_count, salt_value):
    width = KV_HEADS * HEAD_DIM
    noise = jnp.clip(jax.random.normal(jax.random.fold_in(key, salt_value), (row_count, width), jnp.float32), -5.0, 5.0)
    return noise


def draw_cached_keys(key, part):
    return key_draw(key, TOKENS, 11).astype(jnp.bfloat16)


def draw_fresh_keys(key, part):
    return key_draw(key, ROWS, 12).astype(jnp.bfloat16)


def draw_queries(key, part):
    width = HEADS * HEAD_DIM
    noise = jnp.clip(jax.random.normal(jax.random.fold_in(key, 13), (ROWS, width), jnp.float32) * 1.5, -9.0, 9.0)
    return noise.astype(jnp.bfloat16)


def draw_recompute_index(key, part):
    row_keys = jax.random.split(jax.random.fold_in(key, 21), GROUPS)

    def one_row(row_key):
        return jax.random.permutation(row_key, GROUP_LEN)[:R_MAX]
    return jax.vmap(one_row)(row_keys).astype(jnp.int32)


def draw_group_offsets(key, part):
    steps_between = GROUP_LEN + jax.random.randint(jax.random.fold_in(key, 31), (GROUPS,), 0, GROUP_LEN)
    steps_between = jnp.where(jnp.arange(GROUPS) == 0, 0, steps_between).astype(jnp.int32)
    running = jnp.cumsum(steps_between).astype(jnp.int32)
    final_start = (GROUPS - 1) * (2 * GROUP_LEN - 1)
    return (running + (final_start - running[GROUPS - 1])).astype(jnp.int32)


def levels(key, dims, pieces, least, top_value):
    loudness, own = 1.0, jax.random.fold_in(key, 6)
    for position, shards_of in pieces:
        heights = jnp.exp(jax.random.uniform(jax.random.fold_in(own, position), (shards_of,), jnp.float32, least / len(pieces), top_value / len(pieces)))
        loudness = loudness * jnp.repeat(heights, dims[position] // shards_of).reshape([-1 if axis == position else 1 for axis in range(len(dims))])
    return loudness


def profile(count, total, limit, skew):
    loads = [(1 << 20) // math.isqrt(rank ** skew) + 1 for rank in range(2, count + 1)]
    spare, given = total - limit - (count - 1), [1] * (count - 1)
    while spare > 0:
        candidates = [i for i in range(count - 1) if given[i] < limit]
        whole, left = sum([loads[i] for i in candidates]), spare
        for i in candidates:
            more = min(limit - given[i], max(1, left * loads[i] // whole), spare)
            given[i] = given[i] + more
            spare = spare - more
    return np.array([limit] + given)


def uneven(key, count, total, reach, skew):
    if count == 2:
        one = jax.random.randint(key, (), max(1, total - reach), min(reach, total - 1) + 1)
        return jnp.stack([one, total - one])
    sizes = jnp.asarray(profile(count, total, reach, skew), jnp.int32)
    couples = (count - 1) // 2
    source_of, taker = sizes[1:1 + 2 * couples:2], sizes[2:2 + 2 * couples:2]
    slack = jnp.minimum(source_of - 1, reach - taker)
    moved = jax.random.randint(jax.random.fold_in(key, 1), (couples,), 0, 1 << 20) % (slack + 1)
    sizes = sizes.at[1:1 + 2 * couples:2].set(source_of - moved).at[2:2 + 2 * couples:2].set(taker + moved)
    return sizes[jax.random.permutation(jax.random.fold_in(key, 2), count)]


def normal_values(own_key, extent, scale, most, pieces=(), kind=jnp.bfloat16):
    level = levels(own_key, extent, pieces, -0.22, 0.18) if pieces else 1.0
    drawn = jax.random.normal(own_key, extent, jnp.float32) * scale * level
    return jnp.minimum(jnp.maximum(drawn, -most), most).astype(kind)


def setup_inputs(seed: int = 0) -> dict:
    splits = jax.random.split(jax.random.key(seed), 9)
    return {
        "queries": draw_queries(jax.random.fold_in(splits[8], 71), 0),
        "cached_keys": draw_cached_keys(jax.random.fold_in(splits[8], 71), 0),
        "cached_values": normal_values(splits[2], (TOKENS, KV_HEADS * HEAD_DIM), 1.0, 6.0, ((0, 16), (1, 2))),
        "fresh_keys": draw_fresh_keys(jax.random.fold_in(splits[8], 71), 0),
        "fresh_values": normal_values(splits[4], (ROWS, KV_HEADS * HEAD_DIM), 1.0, 6.0, ((0, 16), (1, 2))),
        "recompute_index": draw_recompute_index(jax.random.fold_in(splits[8], 71), 0),
        "recompute_count": uneven(splits[6], GROUPS, GROUPS * R_MAX * 7 // 8, R_MAX, 1).astype(jnp.int32),
        "group_offsets": draw_group_offsets(jax.random.fold_in(splits[8], 71), 0),
    }


def inverse_freq():
    half_dim = HEAD_DIM // 2
    exponent = jnp.arange(half_dim, dtype=jnp.float32) * 2.0 / HEAD_DIM
    base_freq = 1.0 / 500000.0 ** exponent
    wavelength = 2.0 * jnp.pi / base_freq
    smooth = (8192.0 / wavelength - 1.0) / 3.0
    blended_freq = (1.0 - smooth) * base_freq / 8.0 + smooth * base_freq
    return jnp.where(wavelength < 2048.0, base_freq, jnp.where(wavelength > 8192.0, base_freq / 8.0, blended_freq))

def rotate(values, positions):
    row_count = values.shape[0]
    head_count = values.shape[1] // HEAD_DIM
    half_dim = HEAD_DIM // 2
    angles = positions.astype(jnp.float32)[:, None] * inverse_freq()[None, :]
    cosine = jnp.cos(angles)[:, None, :]
    sine_part = jnp.sin(angles)[:, None, :]
    pieces_f = values.astype(jnp.float32).reshape(row_count, head_count, HEAD_DIM)
    first_half = pieces_f[:, :, :half_dim]
    second_half = pieces_f[:, :, half_dim:]
    turned = jnp.concatenate([first_half * cosine - second_half * sine_part, second_half * cosine + first_half * sine_part], axis=2)
    return turned.reshape(row_count, head_count * HEAD_DIM)

def reference(queries, cached_keys, cached_values, fresh_keys, fresh_values, recompute_index, recompute_count, group_offsets):
    heads_per = HEADS // KV_HEADS
    kv_width = KV_HEADS * HEAD_DIM
    positions = jnp.arange(GROUP_LEN, dtype=jnp.int32)
    slot_ids = jnp.arange(R_MAX, dtype=jnp.int32)
    score_scale = 1.0 / math.sqrt(HEAD_DIM)

    def join_group(number):
        start_pos = group_offsets[number]
        key_rows = lax.dynamic_slice_in_dim(cached_keys, (number * GROUP_LEN).astype(jnp.int32), GROUP_LEN, 0)
        value_rows = lax.dynamic_slice_in_dim(cached_values, (number * GROUP_LEN).astype(jnp.int32), GROUP_LEN, 0)
        fresh_key_rows = lax.dynamic_slice_in_dim(fresh_keys, (number * R_MAX).astype(jnp.int32), R_MAX, 0)
        fresh_value_rows = lax.dynamic_slice_in_dim(fresh_values, (number * R_MAX).astype(jnp.int32), R_MAX, 0)
        indices = recompute_index[number]
        live_rows = slot_ids < recompute_count[number]
        turned = rotate(key_rows, start_pos + 0 * positions).astype(jnp.bfloat16)
        fresh_turned = rotate(fresh_key_rows, start_pos + indices).astype(jnp.bfloat16)
        target = jnp.where(live_rows, indices, GROUP_LEN).astype(jnp.int32)
        blended_keys = turned.at[target].set(fresh_turned, mode='drop')
        blended_values = value_rows.at[target].set(fresh_value_rows, mode='drop')
        key_gap = fresh_turned.astype(jnp.float32) - turned[indices].astype(jnp.float32)
        value_gap = fresh_value_rows.astype(jnp.float32) - value_rows[indices].astype(jnp.float32)
        kv_drift = lax.optimization_barrier(jnp.sum(key_gap * key_gap + value_gap * value_gap, axis=1)) / (2.0 * KV_HEADS * HEAD_DIM)
        kv_drift = jnp.where(live_rows, kv_drift, jnp.zeros((), jnp.float32))
        return (blended_keys, blended_values, kv_drift)
    joined_keys, joined_values, drift = lax.map(join_group, jnp.arange(GROUPS, dtype=jnp.int32))
    joined_keys = joined_keys.reshape(TOKENS, kv_width)
    joined_values = joined_values.reshape(TOKENS, kv_width)
    query_pos = (group_offsets[:, None] + recompute_index).reshape(-1)
    turned_queries = rotate(queries, query_pos).astype(jnp.bfloat16)
    query_grid = turned_queries.reshape(GROUPS, R_MAX, KV_HEADS, heads_per, HEAD_DIM)
    key_pos = (group_offsets[:, None] + positions[None, :]).reshape(-1)
    key_grid = joined_keys.reshape(TOKENS, KV_HEADS, HEAD_DIM)
    value_grid = joined_values.reshape(TOKENS, KV_HEADS, HEAD_DIM)
    slot_pos = query_pos.reshape(GROUPS, R_MAX)

    def attend_pair(number):
        group_no = number // KV_HEADS
        kv_head = number % KV_HEADS
        picked = lax.dynamic_index_in_dim(query_grid, group_no, 0, keepdims=False)
        picked = lax.dynamic_index_in_dim(picked, kv_head, 1, keepdims=False).reshape(R_MAX * heads_per, HEAD_DIM)
        key_rows = lax.dynamic_index_in_dim(key_grid, kv_head, 1, keepdims=False)
        value_rows = lax.dynamic_index_in_dim(value_grid, kv_head, 1, keepdims=False)
        row_pos = jnp.repeat(lax.dynamic_index_in_dim(slot_pos, group_no, 0, keepdims=False), heads_per)
        scores = jnp.dot(picked, key_rows.T, preferred_element_type=jnp.float32) * score_scale
        visible = key_pos[None, :] <= row_pos[:, None]
        row_peak = lax.optimization_barrier(jnp.max(jnp.where(visible, scores, -jnp.inf), axis=1, keepdims=True))
        weights = jnp.where(visible, jnp.exp(scores - row_peak), jnp.zeros((), jnp.float32))
        denominator = lax.optimization_barrier(jnp.sum(weights, axis=1, keepdims=True))
        return jnp.dot(weights.astype(jnp.bfloat16), value_rows, preferred_element_type=jnp.float32) / denominator
    blended = lax.map(attend_pair, jnp.arange(GROUPS * KV_HEADS, dtype=jnp.int32))
    blended = blended.reshape(GROUPS, KV_HEADS, R_MAX, heads_per, HEAD_DIM).transpose(0, 2, 1, 3, 4).reshape(ROWS, HEADS * HEAD_DIM)
    live_all = (slot_ids[None, :] < recompute_count[:, None]).reshape(-1)
    attention = jnp.where(live_all[:, None], blended, jnp.zeros((), jnp.float32)).astype(jnp.bfloat16)
    return (attention, joined_keys, joined_values, drift)
```

```python
import functools
import math

import jax
import jax.numpy as jnp
from jax import lax
from jax.experimental import pallas as pl
from jax.experimental.pallas import tpu as pltpu
from jax.sharding import PartitionSpec as P

HEADS = 64
KV_HEADS = 8
HEAD_DIM = 128
HEADS_PER = HEADS // KV_HEADS
SCALE = math.log2(math.e) / math.sqrt(HEAD_DIM)
NEG_FILL = -1e30
LAYERS = 4
MESH = pl.DeviceIdType.MESH


def inverse_freq():
    half_dim = HEAD_DIM // 2
    exponent = jnp.arange(half_dim, dtype=jnp.float32) * 2.0 / HEAD_DIM
    base_freq = 1.0 / 500000.0**exponent
    wavelength = 2.0 * jnp.pi / base_freq
    smooth = (8192.0 / wavelength - 1.0) / 3.0
    blended_freq = (1.0 - smooth) * base_freq / 8.0 + smooth * base_freq
    return jnp.where(
        wavelength < 2048.0,
        base_freq,
        jnp.where(wavelength > 8192.0, base_freq / 8.0, blended_freq),
    )


def dot(a, b, a_dim, b_dim, precision=None):
    return lax.dot_general(
        a,
        b,
        (((a_dim,), (b_dim,)), ((), ())),
        preferred_element_type=jnp.float32,
        precision=precision,
    )


def turn(block, cosine, sine):
    x = block.astype(jnp.float32)
    return (x * cosine + pltpu.roll(x, HEAD_DIM // 2, 1) * sine).astype(jnp.bfloat16)


def kernel(
    n,
    n_head,
    q_ref,
    ck_ref,
    cv_ref,
    fk_ref,
    fv_ref,
    cos_ref,
    sin_ref,
    meta_ref,
    out_ref,
    jk_ref,
    jv_ref,
    drift_ref,
    kv_buf,
    q_all,
    m0,
    l0,
    acc0,
    m1,
    l1,
    acc1,
    po_src,
    ps_src,
    po_dst,
    ps_dst,
    d_buf,
    kv_recv,
    kv_send,
    fw_send,
    q_send,
    q_recv,
    po_send,
    po_recv,
    ps_send,
    ps_recv,
    d_send,
    d_recv,
):
    me = lax.axis_index("ctx")
    my_head = lax.axis_index("head")
    layer_size = n // LAYERS
    half = 2 * layer_size
    columns = layer_size // 2
    kv_local = kv_buf.shape[1]
    tokens = kv_buf.shape[3]
    slots = q_ref.shape[0]
    z = me // layer_size
    odd = z % 2
    mine = me % half
    y = (me % layer_size) // 2
    core = me % 2
    layer_start = z * layer_size
    below_start = layer_start - layer_size
    half_start = me - mine
    sibling = half_start + mine + 1 - 2 * core
    server = layer_size + me % layer_size

    barrier = pltpu.get_barrier_semaphore()

    def greet(target):
        pl.semaphore_signal(barrier, inc=1, device_id={"ctx": target}, device_id_type=MESH)

    greet(sibling)
    other_start = jnp.where(odd == 1, below_start, layer_start + layer_size)
    for k in range(columns):
        if k:
            greet(layer_start + lax.rem(y + k, columns) * 2 + core)
        greet(other_start + k * 2 + core)
    for k in range(1, n_head):
        pl.semaphore_signal(
            barrier,
            inc=1,
            device_id={"head": lax.rem(my_head + k, n_head)},
            device_id_type=MESH,
        )

    @pl.when(z == 1)
    def _():
        greet(me + layer_size)
        greet(me + 2 * layer_size)

    @pl.when(z >= 2)
    def _():
        greet(server)

    idx_row = meta_ref[0:1, :slots]
    live_row = meta_ref[1:2, :slots]
    base_cos = cos_ref[slots : slots + 1, :]
    base_sin = sin_ref[slots : slots + 1, :]
    slot_cos = cos_ref[:slots, :]
    slot_sin = sin_ref[:slots, :]
    hit = lax.broadcasted_iota(jnp.int32, (tokens, slots), 0) == idx_row
    hit_live = hit & (live_row > 0)
    covered = jnp.max(hit_live.astype(jnp.float32), axis=1, keepdims=True) > 0.0
    hit = hit.astype(jnp.bfloat16)
    hit_live = hit_live.astype(jnp.bfloat16)
    ones = jnp.ones((8, HEAD_DIM), jnp.float32)
    drift = jnp.zeros((8, slots), jnp.float32)
    for h in range(kv_local):
        cols = slice(h * HEAD_DIM, (h + 1) * HEAD_DIM)
        turned = turn(ck_ref[:, cols], base_cos, base_sin)
        fresh = turn(fk_ref[:, cols], slot_cos, slot_sin)
        cached_v = cv_ref[:, cols]
        fresh_v = fv_ref[:, cols]
        keys = jnp.where(
            covered, dot(hit_live, fresh, 1, 0), turned.astype(jnp.float32)
        ).astype(jnp.bfloat16)
        vals = jnp.where(
            covered, dot(hit_live, fresh_v, 1, 0), cached_v.astype(jnp.float32)
        ).astype(jnp.bfloat16)
        jk_ref[:, cols] = keys
        jv_ref[:, cols] = vals
        kv_buf[mine, h, 0] = keys
        kv_buf[mine, h, 1] = vals
        key_gap = fresh.astype(jnp.float32) - dot(hit, turned, 0, 0)
        val_gap = fresh_v.astype(jnp.float32) - dot(hit, cached_v, 0, 0)
        drift += dot(
            ones, key_gap * key_gap + val_gap * val_gap, 1, 1, lax.Precision.HIGHEST
        )
        for g in range(HEADS_PER):
            at = (h * HEADS_PER + g) * HEAD_DIM
            q_all[0, h, g * slots : (g + 1) * slots, :] = turn(
                q_ref[:, at : at + HEAD_DIM], slot_cos, slot_sin
            )
    d_buf[my_head] = jnp.zeros(d_buf.shape[1:], jnp.float32)
    d_buf[my_head, :, :slots] = drift

    extra = jnp.where(z == 0, 0, jnp.where(z == 1, 2, 1))
    pl.semaphore_wait(barrier, 2 * columns + n_head - 1 + extra)

    def copy(src, dst, send, recv, target):
        return pltpu.make_async_remote_copy(
            src_ref=src,
            dst_ref=dst,
            send_sem=send,
            recv_sem=recv,
            device_id={"ctx": target},
            device_id_type=MESH,
        )

    def kv_copy(block, h, send, target):
        return copy(kv_buf.at[block, h], kv_buf.at[block, h], send, kv_recv.at[block, h], target)

    def q_copy(h):
        which = jnp.where(z >= 2, z - 1, 1)
        return copy(
            q_all.at[0, h], q_all.at[which, h], q_send.at[h], q_recv.at[which - 1, h], server
        )

    def po_copy(k, h, target):
        return copy(po_src.at[k, h], po_dst.at[h], po_send.at[k, h], po_recv.at[h], target)

    def ps_copy(k, h, target):
        return copy(ps_src.at[k, h], ps_dst.at[h], ps_send.at[k, h], ps_recv.at[h], target)

    def each_send(h, act):
        for k in range(columns):
            @pl.when(odd == 0)
            def _():
                act(kv_copy(mine, h, kv_send.at[columns + k, h],
                            other_start + lax.rem(y + k, columns) * 2 + core))
        for k in range(1, columns):
            there = lax.rem(y + k, columns)

            @pl.when((odd == 1) | (there > y))
            def _():
                act(kv_copy(mine, h, kv_send.at[k, h], layer_start + there * 2 + core))

        @pl.when(z >= 2)
        def _():
            act(q_copy(h))

    def start_sends(h, carry):
        each_send(h, lambda c: c.start())
        return carry

    lax.fori_loop(0, kv_local, start_sends, 0)

    def drift_copy(k):
        target = lax.rem(my_head + k, n_head)
        return pltpu.make_async_remote_copy(
            src_ref=d_buf.at[my_head],
            dst_ref=d_buf.at[my_head],
            send_sem=d_send.at[k],
            recv_sem=d_recv.at[k],
            device_id={"head": target},
            device_id_type=MESH,
        )

    for k in range(1, n_head):
        drift_copy(k).start()

    idx_all = meta_ref[0:1, :]

    def scores(block, h, q):
        return dot(kv_buf[block, h, 0], q, 1, 1) * SCALE

    def update(block, h, s, m, l, acc):
        raised = jnp.maximum(m, jnp.max(s, axis=0, keepdims=True))
        p = jnp.exp2(s - raised)
        shrink = jnp.exp2(m - raised)
        l = l * shrink + jnp.sum(p, axis=0, keepdims=True)
        acc = acc * shrink + dot(kv_buf[block, h, 1], p.astype(jnp.bfloat16), 0, 0)
        return raised, l, acc

    def process(block, h):
        @pl.when(block == mine)
        def _():
            s = scores(block, h, q_all[0, h])
            token = lax.broadcasted_iota(jnp.int32, s.shape, 0)
            s = jnp.where(token <= idx_all, s, NEG_FILL)
            m0[h], l0[h], acc0[h] = update(block, h, s, m0[h], l0[h], acc0[h])

        @pl.when(block < mine)
        def _():
            s = scores(block, h, q_all[0, h])
            m0[h], l0[h], acc0[h] = update(block, h, s, m0[h], l0[h], acc0[h])

        @pl.when(z == 1)
        def _():
            for k in range(2):
                s = scores(block, h, q_all[1 + k, h])
                m1[k], l1[k], acc1[k] = update(block, h, s, m1[k], l1[k], acc1[k])

    def source(j):
        below = j // columns
        there = lax.rem(y + j % columns, columns)
        block = (odd - below) * layer_size + there * 2 + core
        need = ((odd == 1) | (below == 0)) & ((odd == 1) | (there <= y))
        return block, need

    def head_step(h, carry):
        m0[h] = jnp.full(m0.shape[1:], NEG_FILL, jnp.float32)
        l0[h] = jnp.zeros(l0.shape[1:], jnp.float32)
        acc0[h] = jnp.zeros(acc0.shape[1:], jnp.float32)

        @pl.when(z == 1)
        def _():
            m1[...] = jnp.full(m1.shape, NEG_FILL, jnp.float32)
            l1[...] = jnp.zeros(l1.shape, jnp.float32)
            acc1[...] = jnp.zeros(acc1.shape, jnp.float32)
            for k in range(2):
                copy(
                    q_all.at[0, h], q_all.at[1 + k, h], q_send.at[h], q_recv.at[k, h], server
                ).wait_recv()

        def block_step(j, inner):
            block, need = source(j)

            @pl.when(need)
            def _():
                @pl.when(block != mine)
                def _():
                    kv_copy(block, h, fw_send.at[j, h], sibling).wait_recv()

                kv_copy(block, h, fw_send.at[j, h], sibling).start()
                process(block, h)
                twin = block + 1 - 2 * core
                kv_copy(twin, h, fw_send.at[j, h], sibling).wait_recv()
                process(twin, h)

            return inner

        lax.fori_loop(0, 2 * columns, block_step, 0)

        @pl.when(z == 1)
        def _():
            for k in range(2):
                po_src[k, h] = (acc1[k] / l1[k]).astype(jnp.bfloat16)
                ps_src[k, h] = jnp.broadcast_to(m1[k] + jnp.log2(l1[k]), ps_src.shape[2:])
                po_copy(k, h, me + (1 + k) * layer_size).start()
                ps_copy(k, h, me + (1 + k) * layer_size).start()

        return carry

    lax.fori_loop(0, kv_local, head_step, 0)

    live_all = meta_ref[1:2, :] > 0

    def store(h, rows):
        rows = jnp.where(live_all, rows, 0.0).T.astype(jnp.bfloat16)
        for g in range(HEADS_PER):
            at = pl.multiple_of((h * HEADS_PER + g) * HEAD_DIM, HEAD_DIM)
            out_ref[:, pl.ds(at, HEAD_DIM)] = rows[g * slots : (g + 1) * slots, :]

    def finish(h, carry):
        @pl.when(z < 2)
        def _():
            store(h, acc0[h] / l0[h])

        @pl.when(z >= 2)
        def _():
            po_copy(0, h, server).wait_recv()
            ps_copy(0, h, server).wait_recv()
            stat = ps_dst[h, 0:1, :]
            top = jnp.maximum(m0[h], stat)
            own = jnp.exp2(m0[h] - top)
            far = jnp.exp2(stat - top)
            total = l0[h] * own + far
            store(h, acc0[h] * (own / total) + po_dst[h].astype(jnp.float32) * (far / total))

        return carry

    lax.fori_loop(0, kv_local, finish, 0)

    for k in range(1, n_head):
        drift_copy(k).wait_recv()
    summed = d_buf[0, 0:1, :slots]
    for k in range(1, n_head):
        summed = summed + d_buf[k, 0:1, :slots]
    drift_ref[...] = jnp.where(live_row > 0, summed / (2.0 * KV_HEADS * HEAD_DIM), 0.0)
    for k in range(1, n_head):
        drift_copy(k).wait_send()

    def drain(h, carry):
        each_send(h, lambda c: c.wait_send())

        def drain_block(j, inner):
            block, need = source(j)

            @pl.when(need)
            def _():
                kv_copy(block, h, fw_send.at[j, h], sibling).wait_send()

            return inner

        lax.fori_loop(0, 2 * columns, drain_block, 0)

        @pl.when(z == 1)
        def _():
            for k in range(2):
                po_copy(k, h, me + (1 + k) * layer_size).wait_send()
                ps_copy(k, h, me + (1 + k) * layer_size).wait_send()

        return carry

    lax.fori_loop(0, kv_local, drain, 0)


def shards(
    n,
    n_head,
    queries,
    cached_keys,
    cached_values,
    fresh_keys,
    fresh_values,
    recompute_index,
    recompute_count,
    group_offsets,
):
    tokens, width = cached_keys.shape
    slots = queries.shape[0]
    kv_local = width // HEAD_DIM
    own_start = lax.dynamic_index_in_dim(group_offsets, lax.axis_index("ctx"), keepdims=False)
    indices = recompute_index[0]
    live = (jnp.arange(slots, dtype=jnp.int32) < recompute_count[0]).astype(jnp.int32)
    positions = own_start + jnp.concatenate([indices, jnp.zeros((8,), jnp.int32)])
    angles = positions.astype(jnp.float32)[:, None] * inverse_freq()[None, :]
    cosine = jnp.cos(angles)
    sine = jnp.sin(angles)
    cosine = jnp.concatenate([cosine, cosine], axis=1)
    sine = jnp.concatenate([-sine, sine], axis=1)
    meta = jnp.stack([jnp.tile(indices, HEADS_PER), jnp.tile(live, HEADS_PER)])
    rows = slots * HEADS_PER
    half = n // 2
    columns = n // LAYERS // 2
    bf16, f32 = jnp.bfloat16, jnp.float32
    dma = pltpu.SemaphoreType.DMA
    return pl.pallas_call(
        functools.partial(kernel, n, n_head),
        out_shape=(
            jax.ShapeDtypeStruct(queries.shape, bf16),
            jax.ShapeDtypeStruct(cached_keys.shape, bf16),
            jax.ShapeDtypeStruct(cached_values.shape, bf16),
            jax.ShapeDtypeStruct((1, slots), f32),
        ),
        in_specs=[pl.BlockSpec(memory_space=pltpu.VMEM)] * 8,
        out_specs=(pl.BlockSpec(memory_space=pltpu.VMEM),) * 4,
        scratch_shapes=[
            pltpu.VMEM((half, kv_local, 2, tokens, HEAD_DIM), bf16),
            pltpu.VMEM((3, kv_local, rows, HEAD_DIM), bf16),
            pltpu.VMEM((kv_local, 1, rows), f32),
            pltpu.VMEM((kv_local, 1, rows), f32),
            pltpu.VMEM((kv_local, HEAD_DIM, rows), f32),
            pltpu.VMEM((2, 1, rows), f32),
            pltpu.VMEM((2, 1, rows), f32),
            pltpu.VMEM((2, HEAD_DIM, rows), f32),
            pltpu.VMEM((2, kv_local, HEAD_DIM, rows), bf16),
            pltpu.VMEM((2, kv_local, 8, rows), f32),
            pltpu.VMEM((kv_local, HEAD_DIM, rows), bf16),
            pltpu.VMEM((kv_local, 8, rows), f32),
            pltpu.VMEM((n_head, 8, HEAD_DIM), f32),
            dma((half, kv_local)),
            dma((2 * columns, kv_local)),
            dma((2 * columns, kv_local)),
            dma((kv_local,)),
            dma((2, kv_local)),
            dma((2, kv_local)),
            dma((kv_local,)),
            dma((2, kv_local)),
            dma((kv_local,)),
            dma((n_head,)),
            dma((n_head,)),
        ],
        compiler_params=pltpu.CompilerParams(
            collective_id=0, has_side_effects=True, vmem_limit_bytes=40 * 1024 * 1024
        ),
        cost_estimate=pl.CostEstimate(
            flops=4 * half * kv_local * tokens * rows * HEAD_DIM,
            bytes_accessed=8 * tokens * width,
            transcendentals=half * kv_local * tokens * rows,
        ),
    )(queries, cached_keys, cached_values, fresh_keys, fresh_values, cosine, sine, meta)


def solution(mesh):
    return jax.shard_map(
        functools.partial(shards, mesh.shape["ctx"], mesh.shape["head"]),
        mesh=mesh,
        in_specs=(
            P("ctx", "head"),
            P("ctx", "head"),
            P("ctx", "head"),
            P("ctx", "head"),
            P("ctx", "head"),
            P("ctx", None),
            P("ctx"),
            P(),
        ),
        out_specs=(P("ctx", "head"), P("ctx", "head"), P("ctx", "head"), P("ctx", None)),
        check_vma=False,
    )
```

```python
import functools
import math

import jax
import jax.numpy as jnp
from jax import lax
from jax.experimental import pallas as pl
from jax.experimental.pallas import tpu as pltpu
from jax.sharding import PartitionSpec as P

HEADS = 64
KV_HEADS = 8
HEAD_DIM = 128
HEADS_PER = HEADS // KV_HEADS
SCALE = math.log2(math.e) / math.sqrt(HEAD_DIM)
NEG_FILL = -1e30
LAYERS = 4
MESH = pl.DeviceIdType.MESH


def inverse_freq():
    half_dim = HEAD_DIM // 2
    exponent = jnp.arange(half_dim, dtype=jnp.float32) * 2.0 / HEAD_DIM
    base_freq = 1.0 / 500000.0**exponent
    wavelength = 2.0 * jnp.pi / base_freq
    smooth = (8192.0 / wavelength - 1.0) / 3.0
    blended_freq = (1.0 - smooth) * base_freq / 8.0 + smooth * base_freq
    return jnp.where(
        wavelength < 2048.0,
        base_freq,
        jnp.where(wavelength > 8192.0, base_freq / 8.0, blended_freq),
    )


def dot(a, b, a_dim, b_dim, precision=None):
    return lax.dot_general(
        a,
        b,
        (((a_dim,), (b_dim,)), ((), ())),
        preferred_element_type=jnp.float32,
        precision=precision,
    )


def turn(block, cosine, sine):
    x = block.astype(jnp.float32)
    return (x * cosine + pltpu.roll(x, HEAD_DIM // 2, 1) * sine).astype(jnp.bfloat16)


def kernel(
    n,
    n_head,
    q_ref,
    ck_ref,
    cv_ref,
    fk_ref,
    fv_ref,
    cos_ref,
    sin_ref,
    meta_ref,
    wide_ref,
    out_ref,
    jk_ref,
    jv_ref,
    drift_ref,
    kv_buf,
    q_all,
    m0,
    l0,
    acc0,
    m1,
    l1,
    acc1,
    po_src,
    ps_src,
    po_dst,
    ps_dst,
    d_buf,
    kv_recv,
    kv_send,
    fw_send,
    q_send,
    q_recv,
    po_send,
    po_recv,
    ps_send,
    ps_recv,
    d_send,
    d_recv,
):
    me = lax.axis_index("ctx")
    my_head = lax.axis_index("head")
    layer_size = n // LAYERS
    half = 2 * layer_size
    columns = layer_size // 2
    kv_local = kv_buf.shape[1]
    tokens = kv_buf.shape[3]
    slots = q_ref.shape[0]
    z = me // layer_size
    odd = z % 2
    mine = me % half
    y = (me % layer_size) // 2
    core = me % 2
    layer_start = z * layer_size
    below_start = layer_start - layer_size
    half_start = me - mine
    sibling = half_start + mine + 1 - 2 * core
    server = layer_size + me % layer_size

    barrier = pltpu.get_barrier_semaphore()

    def greet(target):
        pl.semaphore_signal(barrier, inc=1, device_id={"ctx": target}, device_id_type=MESH)

    greet(sibling)
    other_start = jnp.where(odd == 1, below_start, layer_start + layer_size)
    for k in range(columns):
        if k:
            greet(layer_start + lax.rem(y + k, columns) * 2 + core)
        greet(other_start + k * 2 + core)
    for k in range(1, n_head):
        pl.semaphore_signal(
            barrier,
            inc=1,
            device_id={"head": lax.rem(my_head + k, n_head)},
            device_id_type=MESH,
        )

    @pl.when(z == 1)
    def _():
        greet(me + layer_size)
        greet(me + 2 * layer_size)

    @pl.when(z >= 2)
    def _():
        greet(server)

    idx_row = meta_ref[0:1, :slots]
    live_row = meta_ref[1:2, :slots]
    base_cos = cos_ref[slots : slots + 1, :]
    base_sin = sin_ref[slots : slots + 1, :]
    slot_cos = cos_ref[:slots, :]
    slot_sin = sin_ref[:slots, :]
    hit = lax.broadcasted_iota(jnp.int32, (tokens, slots), 0) == idx_row
    hit_live = hit & (live_row > 0)
    covered = jnp.max(hit_live.astype(jnp.float32), axis=1, keepdims=True) > 0.0
    hit = hit.astype(jnp.bfloat16)
    hit_live = hit_live.astype(jnp.bfloat16)
    ones = jnp.ones((8, HEAD_DIM), jnp.float32)
    drift = jnp.zeros((8, slots), jnp.float32)
    for h in range(kv_local):
        cols = slice(h * HEAD_DIM, (h + 1) * HEAD_DIM)
        turned = turn(ck_ref[:, cols], base_cos, base_sin)
        fresh = turn(fk_ref[:, cols], slot_cos, slot_sin)
        cached_v = cv_ref[:, cols]
        fresh_v = fv_ref[:, cols]
        keys = jnp.where(
            covered, dot(hit_live, fresh, 1, 0), turned.astype(jnp.float32)
        ).astype(jnp.bfloat16)
        vals = jnp.where(
            covered, dot(hit_live, fresh_v, 1, 0), cached_v.astype(jnp.float32)
        ).astype(jnp.bfloat16)
        jk_ref[:, cols] = keys
        jv_ref[:, cols] = vals
        kv_buf[mine, h, 0] = keys
        kv_buf[mine, h, 1] = vals
        key_gap = fresh.astype(jnp.float32) - dot(hit, turned, 0, 0)
        val_gap = fresh_v.astype(jnp.float32) - dot(hit, cached_v, 0, 0)
        drift += dot(
            ones, key_gap * key_gap + val_gap * val_gap, 1, 1, lax.Precision.HIGHEST
        )
        for g in range(HEADS_PER):
            at = (h * HEADS_PER + g) * HEAD_DIM
            q_all[0, h, g * slots : (g + 1) * slots, :] = turn(
                q_ref[:, at : at + HEAD_DIM], slot_cos, slot_sin
            )
    d_buf[my_head] = jnp.zeros(d_buf.shape[1:], jnp.float32)
    d_buf[my_head, :, :slots] = drift

    extra = jnp.where(z == 0, 0, jnp.where(z == 1, 2, 1))
    pl.semaphore_wait(barrier, 2 * columns + n_head - 1 + extra)

    def copy(src, dst, send, recv, target):
        return pltpu.make_async_remote_copy(
            src_ref=src,
            dst_ref=dst,
            send_sem=send,
            recv_sem=recv,
            device_id={"ctx": target},
            device_id_type=MESH,
        )

    def kv_copy(block, h, send, target):
        return copy(kv_buf.at[block, h], kv_buf.at[block, h], send, kv_recv.at[block, h], target)

    def q_copy(h):
        which = jnp.where(z >= 2, z - 1, 1)
        return copy(
            q_all.at[0, h], q_all.at[which, h], q_send.at[h], q_recv.at[which - 1, h], server
        )

    def po_copy(k, h, target):
        return copy(po_src.at[k, h], po_dst.at[h], po_send.at[k, h], po_recv.at[h], target)

    def ps_copy(k, h, target):
        return copy(ps_src.at[k, h], ps_dst.at[h], ps_send.at[k, h], ps_recv.at[h], target)

    def each_send(h, act):
        for k in range(columns):
            @pl.when(odd == 0)
            def _():
                act(kv_copy(mine, h, kv_send.at[columns + k, h],
                            other_start + lax.rem(y + k, columns) * 2 + core))
        for k in range(1, columns):
            there = lax.rem(y + k, columns)

            @pl.when((odd == 1) | (there > y))
            def _():
                act(kv_copy(mine, h, kv_send.at[k, h], layer_start + there * 2 + core))

        @pl.when(z >= 2)
        def _():
            act(q_copy(h))

    def start_sends(h, carry):
        each_send(h, lambda c: c.start())
        return carry

    lax.fori_loop(0, kv_local, start_sends, 0)

    def drift_copy(k):
        target = lax.rem(my_head + k, n_head)
        return pltpu.make_async_remote_copy(
            src_ref=d_buf.at[my_head],
            dst_ref=d_buf.at[my_head],
            send_sem=d_send.at[k],
            recv_sem=d_recv.at[k],
            device_id={"head": target},
            device_id_type=MESH,
        )

    for k in range(1, n_head):
        drift_copy(k).start()

    idx_all = jnp.concatenate([wide_ref[0]] * HEADS_PER, axis=0)
    repeats = 2 * tokens // HEAD_DIM

    def update(s, v_one, m, l, acc):
        raised = jnp.maximum(m, jnp.max(s, axis=1, keepdims=True))
        p = jnp.exp2(s - jnp.concatenate([raised] * repeats, axis=1)).astype(jnp.bfloat16)
        shrink = jnp.exp2(m - raised)
        both = dot(p, v_one, 1, 0)
        l = l * shrink + both[:, HEAD_DIM:]
        acc = acc * shrink + both[:, :HEAD_DIM]
        return raised, l, acc

    def process(pair, h):
        def operands():
            k = jnp.concatenate([kv_buf[pair, h, 0], kv_buf[pair + 1, h, 0]], axis=0)
            v = jnp.concatenate([kv_buf[pair, h, 1], kv_buf[pair + 1, h, 1]], axis=0)
            return k, jnp.concatenate([v, jnp.ones_like(v)], axis=1)

        def own(k, v_one):
            s = dot(q_all[0, h], k, 1, 1) * SCALE
            token = lax.broadcasted_iota(jnp.int32, s.shape, 1) + (pair - mine) * tokens
            s = jnp.where(token <= jnp.concatenate([idx_all] * repeats, axis=1), s, NEG_FILL)
            m0[h], l0[h], acc0[h] = update(s, v_one, m0[h], l0[h], acc0[h])

        @pl.when((z != 1) & (pair <= mine))
        def _():
            own(*operands())

        @pl.when(z == 1)
        def _():
            k, v_one = operands()
            own(k, v_one)
            for i in range(2):
                s = dot(q_all[1 + i, h], k, 1, 1) * SCALE
                m1[i], l1[i], acc1[i] = update(s, v_one, m1[i], l1[i], acc1[i])

    def source(j):
        below = j // columns
        there = lax.rem(y + j % columns, columns)
        block = (odd - below) * layer_size + there * 2 + core
        need = ((odd == 1) | (below == 0)) & ((odd == 1) | (there <= y))
        return block, need

    def head_step(h, carry):
        m0[h] = jnp.full(m0.shape[1:], NEG_FILL, jnp.float32)
        l0[h] = jnp.zeros(l0.shape[1:], jnp.float32)
        acc0[h] = jnp.zeros(acc0.shape[1:], jnp.float32)

        @pl.when(z == 1)
        def _():
            m1[...] = jnp.full(m1.shape, NEG_FILL, jnp.float32)
            l1[...] = jnp.zeros(l1.shape, jnp.float32)
            acc1[...] = jnp.zeros(acc1.shape, jnp.float32)
            for k in range(2):
                copy(
                    q_all.at[0, h], q_all.at[1 + k, h], q_send.at[h], q_recv.at[k, h], server
                ).wait_recv()

        def block_step(j, inner):
            block, need = source(j)

            @pl.when(need)
            def _():
                @pl.when(block != mine)
                def _():
                    kv_copy(block, h, fw_send.at[j, h], sibling).wait_recv()

                kv_copy(block, h, fw_send.at[j, h], sibling).start()
                twin = block + 1 - 2 * core
                kv_copy(twin, h, fw_send.at[j, h], sibling).wait_recv()
                process(block - core, h)

            return inner

        lax.fori_loop(0, 2 * columns, block_step, 0)

        @pl.when(z == 1)
        def _():
            for k in range(2):
                po_src[k, h] = (acc1[k] / l1[k]).astype(jnp.bfloat16)
                ps_src[k, h] = (m1[k] + jnp.log2(l1[k])).T[:8, :]
                po_copy(k, h, me + (1 + k) * layer_size).start()
                ps_copy(k, h, me + (1 + k) * layer_size).start()

        return carry

    lax.fori_loop(0, kv_local, head_step, 0)

    live_all = jnp.concatenate([wide_ref[1]] * HEADS_PER, axis=0) > 0

    def store(h, rows):
        rows = jnp.where(live_all, rows, 0.0).astype(jnp.bfloat16)
        for g in range(HEADS_PER):
            at = pl.multiple_of((h * HEADS_PER + g) * HEAD_DIM, HEAD_DIM)
            out_ref[:, pl.ds(at, HEAD_DIM)] = rows[g * slots : (g + 1) * slots, :]

    def finish(h, carry):
        @pl.when(z < 2)
        def _():
            store(h, acc0[h] / l0[h])

        @pl.when(z >= 2)
        def _():
            po_copy(0, h, server).wait_recv()
            ps_copy(0, h, server).wait_recv()
            stat = jnp.concatenate([ps_dst[h]] * (HEAD_DIM // 8), axis=0).T
            top = jnp.maximum(m0[h], stat)
            own = jnp.exp2(m0[h] - top)
            far = jnp.exp2(stat - top)
            total = l0[h] * own + far
            store(h, acc0[h] * (own / total) + po_dst[h].astype(jnp.float32) * (far / total))

        return carry

    lax.fori_loop(0, kv_local, finish, 0)

    for k in range(1, n_head):
        drift_copy(k).wait_recv()
    summed = d_buf[0, 0:1, :slots]
    for k in range(1, n_head):
        summed = summed + d_buf[k, 0:1, :slots]
    drift_ref[...] = jnp.where(live_row > 0, summed / (2.0 * KV_HEADS * HEAD_DIM), 0.0)
    for k in range(1, n_head):
        drift_copy(k).wait_send()

    def drain(h, carry):
        each_send(h, lambda c: c.wait_send())

        def drain_block(j, inner):
            block, need = source(j)

            @pl.when(need)
            def _():
                kv_copy(block, h, fw_send.at[j, h], sibling).wait_send()

            return inner

        lax.fori_loop(0, 2 * columns, drain_block, 0)

        @pl.when(z == 1)
        def _():
            for k in range(2):
                po_copy(k, h, me + (1 + k) * layer_size).wait_send()
                ps_copy(k, h, me + (1 + k) * layer_size).wait_send()

        return carry

    lax.fori_loop(0, kv_local, drain, 0)


def shards(
    n,
    n_head,
    queries,
    cached_keys,
    cached_values,
    fresh_keys,
    fresh_values,
    recompute_index,
    recompute_count,
    group_offsets,
):
    tokens, width = cached_keys.shape
    slots = queries.shape[0]
    kv_local = width // HEAD_DIM
    own_start = lax.dynamic_index_in_dim(group_offsets, lax.axis_index("ctx"), keepdims=False)
    indices = recompute_index[0]
    live = (jnp.arange(slots, dtype=jnp.int32) < recompute_count[0]).astype(jnp.int32)
    positions = own_start + jnp.concatenate([indices, jnp.zeros((8,), jnp.int32)])
    angles = positions.astype(jnp.float32)[:, None] * inverse_freq()[None, :]
    cosine = jnp.cos(angles)
    sine = jnp.sin(angles)
    cosine = jnp.concatenate([cosine, cosine], axis=1)
    sine = jnp.concatenate([-sine, sine], axis=1)
    meta = jnp.stack([indices, live])
    wide = jnp.broadcast_to(meta[:, :, None], (2, slots, HEAD_DIM))
    rows = slots * HEADS_PER
    half = n // 2
    columns = n // LAYERS // 2
    bf16, f32 = jnp.bfloat16, jnp.float32
    dma = pltpu.SemaphoreType.DMA
    return pl.pallas_call(
        functools.partial(kernel, n, n_head),
        out_shape=(
            jax.ShapeDtypeStruct(queries.shape, bf16),
            jax.ShapeDtypeStruct(cached_keys.shape, bf16),
            jax.ShapeDtypeStruct(cached_values.shape, bf16),
            jax.ShapeDtypeStruct((1, slots), f32),
        ),
        in_specs=[pl.BlockSpec(memory_space=pltpu.VMEM)] * 9,
        out_specs=(pl.BlockSpec(memory_space=pltpu.VMEM),) * 4,
        scratch_shapes=[
            pltpu.VMEM((half, kv_local, 2, tokens, HEAD_DIM), bf16),
            pltpu.VMEM((3, kv_local, rows, HEAD_DIM), bf16),
            pltpu.VMEM((kv_local, rows, HEAD_DIM), f32),
            pltpu.VMEM((kv_local, rows, HEAD_DIM), f32),
            pltpu.VMEM((kv_local, rows, HEAD_DIM), f32),
            pltpu.VMEM((2, rows, HEAD_DIM), f32),
            pltpu.VMEM((2, rows, HEAD_DIM), f32),
            pltpu.VMEM((2, rows, HEAD_DIM), f32),
            pltpu.VMEM((2, kv_local, rows, HEAD_DIM), bf16),
            pltpu.VMEM((2, kv_local, 8, rows), f32),
            pltpu.VMEM((kv_local, rows, HEAD_DIM), bf16),
            pltpu.VMEM((kv_local, 8, rows), f32),
            pltpu.VMEM((n_head, 8, HEAD_DIM), f32),
            dma((half, kv_local)),
            dma((2 * columns, kv_local)),
            dma((2 * columns, kv_local)),
            dma((kv_local,)),
            dma((2, kv_local)),
            dma((2, kv_local)),
            dma((kv_local,)),
            dma((2, kv_local)),
            dma((kv_local,)),
            dma((n_head,)),
            dma((n_head,)),
        ],
        compiler_params=pltpu.CompilerParams(
            collective_id=0, has_side_effects=True, vmem_limit_bytes=40 * 1024 * 1024
        ),
        cost_estimate=pl.CostEstimate(
            flops=4 * half * kv_local * tokens * rows * HEAD_DIM,
            bytes_accessed=8 * tokens * width,
            transcendentals=half * kv_local * tokens * rows,
        ),
    )(queries, cached_keys, cached_values, fresh_keys, fresh_values, cosine, sine, meta, wide)


def solution(mesh):
    return jax.shard_map(
        functools.partial(shards, mesh.shape["ctx"], mesh.shape["head"]),
        mesh=mesh,
        in_specs=(
            P("ctx", "head"),
            P("ctx", "head"),
            P("ctx", "head"),
            P("ctx", "head"),
            P("ctx", "head"),
            P("ctx", None),
            P("ctx"),
            P(),
        ),
        out_specs=(P("ctx", "head"), P("ctx", "head"), P("ctx", "head"), P("ctx", None)),
        check_vma=False,
    )
```

```python
import functools
import math

import jax
import jax.numpy as jnp
from jax import lax
from jax.experimental import pallas as pl
from jax.experimental.pallas import tpu as pltpu
from jax.sharding import PartitionSpec as P

HEADS = 64
KV_HEADS = 8
HEAD_DIM = 128
HEADS_PER = HEADS // KV_HEADS
SCALE = math.log2(math.e) / math.sqrt(HEAD_DIM)
NEG_FILL = -1e30
LAYERS = 4
MESH = pl.DeviceIdType.MESH


def inverse_freq():
    half_dim = HEAD_DIM // 2
    exponent = jnp.arange(half_dim, dtype=jnp.float32) * 2.0 / HEAD_DIM
    base_freq = 1.0 / 500000.0**exponent
    wavelength = 2.0 * jnp.pi / base_freq
    smooth = (8192.0 / wavelength - 1.0) / 3.0
    blended_freq = (1.0 - smooth) * base_freq / 8.0 + smooth * base_freq
    return jnp.where(
        wavelength < 2048.0,
        base_freq,
        jnp.where(wavelength > 8192.0, base_freq / 8.0, blended_freq),
    )


def dot(a, b, a_dim, b_dim, precision=None):
    return lax.dot_general(
        a,
        b,
        (((a_dim,), (b_dim,)), ((), ())),
        preferred_element_type=jnp.float32,
        precision=precision,
    )


def turn(block, cosine, sine):
    x = block.astype(jnp.float32)
    return (x * cosine + pltpu.roll(x, HEAD_DIM // 2, 1) * sine).astype(jnp.bfloat16)


def kernel(
    n,
    n_head,
    q_ref,
    ck_ref,
    cv_ref,
    fk_ref,
    fv_ref,
    cos_ref,
    sin_ref,
    meta_ref,
    wide_ref,
    out_ref,
    jk_ref,
    jv_ref,
    drift_ref,
    kv_buf,
    q_all,
    m0,
    l0,
    acc0,
    m1,
    l1,
    acc1,
    po_src,
    ps_src,
    po_dst,
    ps_dst,
    d_buf,
    kv_recv,
    kv_send,
    fw_send,
    q_send,
    q_recv,
    po_send,
    po_recv,
    ps_send,
    ps_recv,
    d_send,
    d_recv,
):
    me = lax.axis_index("ctx")
    my_head = lax.axis_index("head")
    layer_size = n // LAYERS
    half = 2 * layer_size
    columns = layer_size // 2
    kv_local = kv_buf.shape[1]
    tokens = kv_buf.shape[3]
    slots = q_ref.shape[0]
    z = me // layer_size
    odd = z % 2
    mine = me % half
    y = (me % layer_size) // 2
    core = me % 2
    layer_start = z * layer_size
    below_start = layer_start - layer_size
    half_start = me - mine
    sibling = half_start + mine + 1 - 2 * core
    server = layer_size + me % layer_size

    barrier = pltpu.get_barrier_semaphore()

    def greet(target):
        pl.semaphore_signal(barrier, inc=1, device_id={"ctx": target}, device_id_type=MESH)

    greet(sibling)
    other_start = jnp.where(odd == 1, below_start, layer_start + layer_size)
    for k in range(columns):
        if k:
            greet(layer_start + lax.rem(y + k, columns) * 2 + core)
        greet(other_start + k * 2 + core)
    for k in range(1, n_head):
        pl.semaphore_signal(
            barrier,
            inc=1,
            device_id={"head": lax.rem(my_head + k, n_head)},
            device_id_type=MESH,
        )

    @pl.when(z == 1)
    def _():
        greet(me + layer_size)
        greet(me + 2 * layer_size)

    @pl.when(z >= 2)
    def _():
        greet(server)

    def copy(src, dst, send, recv, target):
        return pltpu.make_async_remote_copy(
            src_ref=src,
            dst_ref=dst,
            send_sem=send,
            recv_sem=recv,
            device_id={"ctx": target},
            device_id_type=MESH,
        )

    def kv_copy(block, h, send, target):
        return copy(kv_buf.at[block, h], kv_buf.at[block, h], send, kv_recv.at[block, h], target)

    def q_copy(h):
        which = jnp.where(z >= 2, z - 1, 1)
        return copy(
            q_all.at[0, h], q_all.at[which, h], q_send.at[h], q_recv.at[which - 1, h], server
        )

    def po_copy(k, h, target):
        return copy(po_src.at[k, h], po_dst.at[h], po_send.at[k, h], po_recv.at[h], target)

    def ps_copy(k, h, target):
        return copy(ps_src.at[k, h], ps_dst.at[h], ps_send.at[k, h], ps_recv.at[h], target)

    def each_send(h, act):
        for k in range(columns):
            @pl.when(odd == 0)
            def _():
                act(kv_copy(mine, h, kv_send.at[columns + k, h],
                            other_start + lax.rem(y + k, columns) * 2 + core))
        for k in range(1, columns):
            there = lax.rem(y + k, columns)

            @pl.when((odd == 1) | (there > y))
            def _():
                act(kv_copy(mine, h, kv_send.at[k, h], layer_start + there * 2 + core))

    idx_row = meta_ref[0:1, :slots]
    live_row = meta_ref[1:2, :slots]
    base_cos = cos_ref[slots : slots + 1, :]
    base_sin = sin_ref[slots : slots + 1, :]
    slot_cos = cos_ref[:slots, :]
    slot_sin = sin_ref[:slots, :]
    hit = lax.broadcasted_iota(jnp.int32, (tokens, slots), 0) == idx_row
    hit_live = hit & (live_row > 0)
    covered = jnp.max(hit_live.astype(jnp.float32), axis=1, keepdims=True) > 0.0
    hit = hit.astype(jnp.bfloat16)
    hit_live = hit_live.astype(jnp.bfloat16)
    ones = jnp.ones((8, HEAD_DIM), jnp.float32)
    drift = jnp.zeros((8, slots), jnp.float32)
    turned_rows, fresh_rows = [], []
    for h in range(kv_local):
        cols = slice(h * HEAD_DIM, (h + 1) * HEAD_DIM)
        turned = turn(ck_ref[:, cols], base_cos, base_sin)
        fresh = turn(fk_ref[:, cols], slot_cos, slot_sin)
        cached_v = cv_ref[:, cols]
        fresh_v = fv_ref[:, cols]
        keys = jnp.where(
            covered, dot(hit_live, fresh, 1, 0), turned.astype(jnp.float32)
        ).astype(jnp.bfloat16)
        vals = jnp.where(
            covered, dot(hit_live, fresh_v, 1, 0), cached_v.astype(jnp.float32)
        ).astype(jnp.bfloat16)
        jk_ref[:, cols] = keys
        jv_ref[:, cols] = vals
        kv_buf[mine, h, 0] = keys
        kv_buf[mine, h, 1] = vals
        if h == 0:
            extra = jnp.where(z == 0, 0, jnp.where(z == 1, 2, 1))
            pl.semaphore_wait(barrier, 2 * columns + n_head - 1 + extra)
        each_send(h, lambda c: c.start())
        turned_rows.append(turned)
        fresh_rows.append(fresh)
    for h in range(kv_local):
        cols = slice(h * HEAD_DIM, (h + 1) * HEAD_DIM)
        turned, fresh = turned_rows[h], fresh_rows[h]
        cached_v, fresh_v = cv_ref[:, cols], fv_ref[:, cols]
        key_gap = fresh.astype(jnp.float32) - dot(hit, turned, 0, 0)
        val_gap = fresh_v.astype(jnp.float32) - dot(hit, cached_v, 0, 0)
        drift += dot(
            ones, key_gap * key_gap + val_gap * val_gap, 1, 1, lax.Precision.HIGHEST
        )
        for g in range(HEADS_PER):
            at = (h * HEADS_PER + g) * HEAD_DIM
            q_all[0, h, g * slots : (g + 1) * slots, :] = turn(
                q_ref[:, at : at + HEAD_DIM], slot_cos, slot_sin
            )

        @pl.when(z >= 2)
        def _():
            q_copy(h).start()

    d_buf[my_head] = jnp.zeros(d_buf.shape[1:], jnp.float32)
    d_buf[my_head, :, :slots] = drift

    def drift_copy(k):
        target = lax.rem(my_head + k, n_head)
        return pltpu.make_async_remote_copy(
            src_ref=d_buf.at[my_head],
            dst_ref=d_buf.at[my_head],
            send_sem=d_send.at[k],
            recv_sem=d_recv.at[k],
            device_id={"head": target},
            device_id_type=MESH,
        )

    for k in range(1, n_head):
        drift_copy(k).start()

    idx_all = jnp.concatenate([wide_ref[0]] * HEADS_PER, axis=0)
    repeats = 2 * tokens // HEAD_DIM

    def update(s, v_one, m, l, acc):
        raised = jnp.maximum(m, jnp.max(s, axis=1, keepdims=True))
        p = jnp.exp2(s - jnp.concatenate([raised] * repeats, axis=1)).astype(jnp.bfloat16)
        shrink = jnp.exp2(m - raised)
        both = dot(p, v_one, 1, 0)
        l = l * shrink + both[:, HEAD_DIM:]
        acc = acc * shrink + both[:, :HEAD_DIM]
        return raised, l, acc

    def process(pair, h):
        def operands():
            k = jnp.concatenate([kv_buf[pair, h, 0], kv_buf[pair + 1, h, 0]], axis=0)
            v = jnp.concatenate([kv_buf[pair, h, 1], kv_buf[pair + 1, h, 1]], axis=0)
            return k, jnp.concatenate([v, jnp.ones_like(v)], axis=1)

        def own(k, v_one):
            s = dot(q_all[0, h], k, 1, 1) * SCALE
            token = lax.broadcasted_iota(jnp.int32, s.shape, 1) + (pair - mine) * tokens
            s = jnp.where(token <= jnp.concatenate([idx_all] * repeats, axis=1), s, NEG_FILL)
            m0[h], l0[h], acc0[h] = update(s, v_one, m0[h], l0[h], acc0[h])

        @pl.when((z != 1) & (pair <= mine))
        def _():
            own(*operands())

        @pl.when(z == 1)
        def _():
            k, v_one = operands()
            own(k, v_one)
            for i in range(2):
                s = dot(q_all[1 + i, h], k, 1, 1) * SCALE
                m1[i], l1[i], acc1[i] = update(s, v_one, m1[i], l1[i], acc1[i])

    def source(j):
        below = j // columns
        there = lax.rem(y + j % columns, columns)
        block = (odd - below) * layer_size + there * 2 + core
        need = ((odd == 1) | (below == 0)) & ((odd == 1) | (there <= y))
        return block, need

    steps = 2 * columns

    def advance(t):
        h, j = t // steps, t % steps
        block, need = source(j)

        @pl.when(need)
        def _():
            @pl.when(block != mine)
            def _():
                kv_copy(block, h, fw_send.at[j, h], sibling).wait_recv()

            kv_copy(block, h, fw_send.at[j, h], sibling).start()

    def attend_step(t, carry):
        h, j = t // steps, t % steps

        @pl.when(t + 1 < kv_local * steps)
        def _():
            advance(t + 1)

        @pl.when(j == 0)
        def _():
            m0[h] = jnp.full(m0.shape[1:], NEG_FILL, jnp.float32)
            l0[h] = jnp.zeros(l0.shape[1:], jnp.float32)
            acc0[h] = jnp.zeros(acc0.shape[1:], jnp.float32)

            @pl.when(z == 1)
            def _():
                m1[...] = jnp.full(m1.shape, NEG_FILL, jnp.float32)
                l1[...] = jnp.zeros(l1.shape, jnp.float32)
                acc1[...] = jnp.zeros(acc1.shape, jnp.float32)
                for k in range(2):
                    copy(
                        q_all.at[0, h], q_all.at[1 + k, h], q_send.at[h], q_recv.at[k, h], server
                    ).wait_recv()

        block, need = source(j)

        @pl.when(need)
        def _():
            twin = block + 1 - 2 * core
            kv_copy(twin, h, fw_send.at[j, h], sibling).wait_recv()
            process(block - core, h)

        @pl.when((z == 1) & (j == steps - 1))
        def _():
            for k in range(2):
                po_src[k, h] = (acc1[k] / l1[k]).astype(jnp.bfloat16)
                ps_src[k, h] = (m1[k] + jnp.log2(l1[k])).T[:8, :]
                po_copy(k, h, me + (1 + k) * layer_size).start()
                ps_copy(k, h, me + (1 + k) * layer_size).start()

        return carry

    advance(jnp.int32(0))
    lax.fori_loop(0, kv_local * steps, attend_step, 0)

    live_all = jnp.concatenate([wide_ref[1]] * HEADS_PER, axis=0) > 0

    def store(h, rows):
        rows = jnp.where(live_all, rows, 0.0).astype(jnp.bfloat16)
        for g in range(HEADS_PER):
            at = pl.multiple_of((h * HEADS_PER + g) * HEAD_DIM, HEAD_DIM)
            out_ref[:, pl.ds(at, HEAD_DIM)] = rows[g * slots : (g + 1) * slots, :]

    def finish(h, carry):
        @pl.when(z < 2)
        def _():
            store(h, acc0[h] / l0[h])

        @pl.when(z >= 2)
        def _():
            po_copy(0, h, server).wait_recv()
            ps_copy(0, h, server).wait_recv()
            stat = jnp.concatenate([ps_dst[h]] * (HEAD_DIM // 8), axis=0).T
            top = jnp.maximum(m0[h], stat)
            own = jnp.exp2(m0[h] - top)
            far = jnp.exp2(stat - top)
            total = l0[h] * own + far
            store(h, acc0[h] * (own / total) + po_dst[h].astype(jnp.float32) * (far / total))

        return carry

    lax.fori_loop(0, kv_local, finish, 0)

    for k in range(1, n_head):
        drift_copy(k).wait_recv()
    summed = d_buf[0, 0:1, :slots]
    for k in range(1, n_head):
        summed = summed + d_buf[k, 0:1, :slots]
    drift_ref[...] = jnp.where(live_row > 0, summed / (2.0 * KV_HEADS * HEAD_DIM), 0.0)
    for k in range(1, n_head):
        drift_copy(k).wait_send()

    def drain(h, carry):
        each_send(h, lambda c: c.wait_send())

        @pl.when(z >= 2)
        def _():
            q_copy(h).wait_send()

        def drain_block(j, inner):
            block, need = source(j)

            @pl.when(need)
            def _():
                kv_copy(block, h, fw_send.at[j, h], sibling).wait_send()

            return inner

        lax.fori_loop(0, 2 * columns, drain_block, 0)

        @pl.when(z == 1)
        def _():
            for k in range(2):
                po_copy(k, h, me + (1 + k) * layer_size).wait_send()
                ps_copy(k, h, me + (1 + k) * layer_size).wait_send()

        return carry

    lax.fori_loop(0, kv_local, drain, 0)


def shards(
    n,
    n_head,
    queries,
    cached_keys,
    cached_values,
    fresh_keys,
    fresh_values,
    recompute_index,
    recompute_count,
    group_offsets,
):
    tokens, width = cached_keys.shape
    slots = queries.shape[0]
    kv_local = width // HEAD_DIM
    own_start = lax.dynamic_index_in_dim(group_offsets, lax.axis_index("ctx"), keepdims=False)
    indices = recompute_index[0]
    live = (jnp.arange(slots, dtype=jnp.int32) < recompute_count[0]).astype(jnp.int32)
    positions = own_start + jnp.concatenate([indices, jnp.zeros((8,), jnp.int32)])
    angles = positions.astype(jnp.float32)[:, None] * inverse_freq()[None, :]
    cosine = jnp.cos(angles)
    sine = jnp.sin(angles)
    cosine = jnp.concatenate([cosine, cosine], axis=1)
    sine = jnp.concatenate([-sine, sine], axis=1)
    meta = jnp.stack([indices, live])
    wide = jnp.broadcast_to(meta[:, :, None], (2, slots, HEAD_DIM))
    rows = slots * HEADS_PER
    half = n // 2
    columns = n // LAYERS // 2
    bf16, f32 = jnp.bfloat16, jnp.float32
    dma = pltpu.SemaphoreType.DMA
    return pl.pallas_call(
        functools.partial(kernel, n, n_head),
        out_shape=(
            jax.ShapeDtypeStruct(queries.shape, bf16),
            jax.ShapeDtypeStruct(cached_keys.shape, bf16),
            jax.ShapeDtypeStruct(cached_values.shape, bf16),
            jax.ShapeDtypeStruct((1, slots), f32),
        ),
        in_specs=[pl.BlockSpec(memory_space=pltpu.VMEM)] * 9,
        out_specs=(pl.BlockSpec(memory_space=pltpu.VMEM),) * 4,
        scratch_shapes=[
            pltpu.VMEM((half, kv_local, 2, tokens, HEAD_DIM), bf16),
            pltpu.VMEM((3, kv_local, rows, HEAD_DIM), bf16),
            pltpu.VMEM((kv_local, rows, HEAD_DIM), f32),
            pltpu.VMEM((kv_local, rows, HEAD_DIM), f32),
            pltpu.VMEM((kv_local, rows, HEAD_DIM), f32),
            pltpu.VMEM((2, rows, HEAD_DIM), f32),
            pltpu.VMEM((2, rows, HEAD_DIM), f32),
            pltpu.VMEM((2, rows, HEAD_DIM), f32),
            pltpu.VMEM((2, kv_local, rows, HEAD_DIM), bf16),
            pltpu.VMEM((2, kv_local, 8, rows), f32),
            pltpu.VMEM((kv_local, rows, HEAD_DIM), bf16),
            pltpu.VMEM((kv_local, 8, rows), f32),
            pltpu.VMEM((n_head, 8, HEAD_DIM), f32),
            dma((half, kv_local)),
            dma((2 * columns, kv_local)),
            dma((2 * columns, kv_local)),
            dma((kv_local,)),
            dma((2, kv_local)),
            dma((2, kv_local)),
            dma((kv_local,)),
            dma((2, kv_local)),
            dma((kv_local,)),
            dma((n_head,)),
            dma((n_head,)),
        ],
        compiler_params=pltpu.CompilerParams(
            collective_id=0, has_side_effects=True, vmem_limit_bytes=40 * 1024 * 1024
        ),
        cost_estimate=pl.CostEstimate(
            flops=4 * half * kv_local * tokens * rows * HEAD_DIM,
            bytes_accessed=8 * tokens * width,
            transcendentals=half * kv_local * tokens * rows,
        ),
    )(queries, cached_keys, cached_values, fresh_keys, fresh_values, cosine, sine, meta, wide)


def solution(mesh):
    return jax.shard_map(
        functools.partial(shards, mesh.shape["ctx"], mesh.shape["head"]),
        mesh=mesh,
        in_specs=(
            P("ctx", "head"),
            P("ctx", "head"),
            P("ctx", "head"),
            P("ctx", "head"),
            P("ctx", "head"),
            P("ctx", None),
            P("ctx"),
            P(),
        ),
        out_specs=(P("ctx", "head"), P("ctx", "head"), P("ctx", "head"), P("ctx", None)),
        check_vma=False,
    )
```

```python
import functools
import math

import jax
import jax.numpy as jnp
from jax import lax
from jax.experimental import pallas as pl
from jax.experimental.pallas import tpu as pltpu
from jax.sharding import PartitionSpec as P

HEADS = 64
KV_HEADS = 8
HEAD_DIM = 128
HEADS_PER = HEADS // KV_HEADS
SCALE = math.log2(math.e) / math.sqrt(HEAD_DIM)
NEG_FILL = -1e30
LAYERS = 4
MESH = pl.DeviceIdType.MESH


def inverse_freq():
    half_dim = HEAD_DIM // 2
    exponent = jnp.arange(half_dim, dtype=jnp.float32) * 2.0 / HEAD_DIM
    base_freq = 1.0 / 500000.0**exponent
    wavelength = 2.0 * jnp.pi / base_freq
    smooth = (8192.0 / wavelength - 1.0) / 3.0
    blended_freq = (1.0 - smooth) * base_freq / 8.0 + smooth * base_freq
    return jnp.where(
        wavelength < 2048.0,
        base_freq,
        jnp.where(wavelength > 8192.0, base_freq / 8.0, blended_freq),
    )


def dot(a, b, a_dim, b_dim, precision=None):
    return lax.dot_general(
        a,
        b,
        (((a_dim,), (b_dim,)), ((), ())),
        preferred_element_type=jnp.float32,
        precision=precision,
    )


def turn(block, cosine, sine):
    x = block.astype(jnp.float32)
    return (x * cosine + pltpu.roll(x, HEAD_DIM // 2, 1) * sine).astype(jnp.bfloat16)


def kernel(
    n,
    n_head,
    q_ref,
    ck_ref,
    cv_ref,
    fk_ref,
    fv_ref,
    cos_ref,
    sin_ref,
    meta_ref,
    wide_ref,
    out_ref,
    jk_ref,
    jv_ref,
    drift_ref,
    kv_buf,
    q_all,
    m0,
    l0,
    acc0,
    m1,
    l1,
    acc1,
    po_src,
    ps_src,
    po_dst,
    ps_dst,
    d_buf,
    kv_recv,
    kv_send,
    fw_send,
    q_send,
    q_recv,
    po_send,
    po_recv,
    ps_send,
    ps_recv,
    d_send,
    d_recv,
):
    me = lax.axis_index("ctx")
    my_head = lax.axis_index("head")
    layer_size = n // LAYERS
    half = 2 * layer_size
    columns = layer_size // 2
    kv_local = kv_buf.shape[1]
    tokens = kv_buf.shape[3]
    slots = q_ref.shape[0]
    z = me // layer_size
    odd = z % 2
    mine = me % half
    y = (me % layer_size) // 2
    core = me % 2
    layer_start = z * layer_size
    below_start = layer_start - layer_size
    half_start = me - mine
    sibling = half_start + mine + 1 - 2 * core
    partner = lax.rem(me + half, n)
    serves = z < 2
    full = z != 2

    barrier = pltpu.get_barrier_semaphore()

    def greet(target):
        pl.semaphore_signal(barrier, inc=1, device_id={"ctx": target}, device_id_type=MESH)

    greet(sibling)
    other_start = jnp.where(odd == 1, below_start, layer_start + layer_size)
    for k in range(columns):
        if k:
            greet(layer_start + lax.rem(y + k, columns) * 2 + core)
        greet(other_start + k * 2 + core)
    for k in range(1, n_head):
        pl.semaphore_signal(
            barrier,
            inc=1,
            device_id={"head": lax.rem(my_head + k, n_head)},
            device_id_type=MESH,
        )

    greet(partner)

    def copy(src, dst, send, recv, target):
        return pltpu.make_async_remote_copy(
            src_ref=src,
            dst_ref=dst,
            send_sem=send,
            recv_sem=recv,
            device_id={"ctx": target},
            device_id_type=MESH,
        )

    def kv_copy(block, h, send, target):
        return copy(kv_buf.at[block, h], kv_buf.at[block, h], send, kv_recv.at[block, h], target)

    def q_copy(h):
        return copy(q_all.at[0, h], q_all.at[1, h], q_send.at[h], q_recv.at[h], partner)

    def po_copy(h):
        return copy(po_src.at[h], po_dst.at[h], po_send.at[h], po_recv.at[h], partner)

    def ps_copy(h):
        return copy(ps_src.at[h], ps_dst.at[h], ps_send.at[h], ps_recv.at[h], partner)

    def each_send(h, act):
        for k in range(columns):
            @pl.when(z != 3)
            def _():
                act(kv_copy(mine, h, kv_send.at[columns + k, h],
                            other_start + lax.rem(y + k, columns) * 2 + core))
        for k in range(1, columns):
            there = lax.rem(y + k, columns)

            @pl.when(full | (there > y))
            def _():
                act(kv_copy(mine, h, kv_send.at[k, h], layer_start + there * 2 + core))

    idx_row = meta_ref[0:1, :slots]
    live_row = meta_ref[1:2, :slots]
    base_cos = cos_ref[slots : slots + 1, :]
    base_sin = sin_ref[slots : slots + 1, :]
    slot_cos = cos_ref[:slots, :]
    slot_sin = sin_ref[:slots, :]
    hit = lax.broadcasted_iota(jnp.int32, (tokens, slots), 0) == idx_row
    hit_live = hit & (live_row > 0)
    covered = jnp.max(hit_live.astype(jnp.float32), axis=1, keepdims=True) > 0.0
    hit = hit.astype(jnp.bfloat16)
    hit_live = hit_live.astype(jnp.bfloat16)
    ones = jnp.ones((8, HEAD_DIM), jnp.float32)
    drift = jnp.zeros((8, slots), jnp.float32)
    turned_rows, fresh_rows = [], []
    for h in range(kv_local):
        cols = slice(h * HEAD_DIM, (h + 1) * HEAD_DIM)
        turned = turn(ck_ref[:, cols], base_cos, base_sin)
        fresh = turn(fk_ref[:, cols], slot_cos, slot_sin)
        cached_v = cv_ref[:, cols]
        fresh_v = fv_ref[:, cols]
        keys = jnp.where(
            covered, dot(hit_live, fresh, 1, 0), turned.astype(jnp.float32)
        ).astype(jnp.bfloat16)
        vals = jnp.where(
            covered, dot(hit_live, fresh_v, 1, 0), cached_v.astype(jnp.float32)
        ).astype(jnp.bfloat16)
        jk_ref[:, cols] = keys
        jv_ref[:, cols] = vals
        kv_buf[mine, h, 0] = keys
        kv_buf[mine, h, 1] = vals
        if h == 0:
            pl.semaphore_wait(barrier, 2 * columns + n_head)
        each_send(h, lambda c: c.start())
        turned_rows.append(turned)
        fresh_rows.append(fresh)
    for h in range(kv_local):
        cols = slice(h * HEAD_DIM, (h + 1) * HEAD_DIM)
        turned, fresh = turned_rows[h], fresh_rows[h]
        cached_v, fresh_v = cv_ref[:, cols], fv_ref[:, cols]
        key_gap = fresh.astype(jnp.float32) - dot(hit, turned, 0, 0)
        val_gap = fresh_v.astype(jnp.float32) - dot(hit, cached_v, 0, 0)
        drift += dot(
            ones, key_gap * key_gap + val_gap * val_gap, 1, 1, lax.Precision.HIGHEST
        )
        for g in range(HEADS_PER):
            at = (h * HEADS_PER + g) * HEAD_DIM
            q_all[0, h, g * slots : (g + 1) * slots, :] = turn(
                q_ref[:, at : at + HEAD_DIM], slot_cos, slot_sin
            )

        @pl.when(z >= 2)
        def _():
            q_copy(h).start()

    d_buf[my_head] = jnp.zeros(d_buf.shape[1:], jnp.float32)
    d_buf[my_head, :, :slots] = drift

    def drift_copy(k):
        target = lax.rem(my_head + k, n_head)
        return pltpu.make_async_remote_copy(
            src_ref=d_buf.at[my_head],
            dst_ref=d_buf.at[my_head],
            send_sem=d_send.at[k],
            recv_sem=d_recv.at[k],
            device_id={"head": target},
            device_id_type=MESH,
        )

    for k in range(1, n_head):
        drift_copy(k).start()

    idx_all = jnp.concatenate([wide_ref[0]] * HEADS_PER, axis=0)
    repeats = 2 * tokens // HEAD_DIM

    def update(s, v_one, m, l, acc):
        raised = jnp.maximum(m, jnp.max(s, axis=1, keepdims=True))
        p = jnp.exp2(s - jnp.concatenate([raised] * repeats, axis=1)).astype(jnp.bfloat16)
        shrink = jnp.exp2(m - raised)
        both = dot(p, v_one, 1, 0)
        l = l * shrink + both[:, HEAD_DIM:]
        acc = acc * shrink + both[:, :HEAD_DIM]
        return raised, l, acc

    def process(pair, h):
        def operands():
            k = jnp.concatenate([kv_buf[pair, h, 0], kv_buf[pair + 1, h, 0]], axis=0)
            v = jnp.concatenate([kv_buf[pair, h, 1], kv_buf[pair + 1, h, 1]], axis=0)
            return k, jnp.concatenate([v, jnp.ones_like(v)], axis=1)

        def own(k, v_one):
            s = dot(q_all[0, h], k, 1, 1) * SCALE
            token = lax.broadcasted_iota(jnp.int32, s.shape, 1) + (pair - mine) * tokens
            s = jnp.where(token <= jnp.concatenate([idx_all] * repeats, axis=1), s, NEG_FILL)
            m0[h], l0[h], acc0[h] = update(s, v_one, m0[h], l0[h], acc0[h])

        def served(k, v_one):
            s = dot(q_all[1, h], k, 1, 1) * SCALE
            m1[...], l1[...], acc1[...] = update(s, v_one, m1[...], l1[...], acc1[...])

        @pl.when((z >= 2) & (pair <= mine))
        def _():
            own(*operands())

        @pl.when(serves & (pair <= mine))
        def _():
            k, v_one = operands()
            own(k, v_one)
            served(k, v_one)

        @pl.when(serves & (pair > mine))
        def _():
            served(*operands())

    def source(j):
        below = j // columns
        there = lax.rem(y + j % columns, columns)
        block = jnp.where(below == 0, odd, 1 - odd) * layer_size + there * 2 + core
        need = full | ((below == 0) & (there <= y))
        return block, need

    steps = 2 * columns

    def advance(t):
        h, j = t // steps, t % steps
        block, need = source(j)

        @pl.when(need)
        def _():
            @pl.when(block != mine)
            def _():
                kv_copy(block, h, fw_send.at[j, h], sibling).wait_recv()

            kv_copy(block, h, fw_send.at[j, h], sibling).start()

    def attend_step(t, carry):
        h, j = t // steps, t % steps

        @pl.when(t + 1 < kv_local * steps)
        def _():
            advance(t + 1)

        @pl.when(j == 0)
        def _():
            m0[h] = jnp.full(m0.shape[1:], NEG_FILL, jnp.float32)
            l0[h] = jnp.zeros(l0.shape[1:], jnp.float32)
            acc0[h] = jnp.zeros(acc0.shape[1:], jnp.float32)

            @pl.when(serves)
            def _():
                m1[...] = jnp.full(m1.shape, NEG_FILL, jnp.float32)
                l1[...] = jnp.zeros(l1.shape, jnp.float32)
                acc1[...] = jnp.zeros(acc1.shape, jnp.float32)
                q_copy(h).wait_recv()

        block, need = source(j)

        @pl.when(need)
        def _():
            twin = block + 1 - 2 * core
            kv_copy(twin, h, fw_send.at[j, h], sibling).wait_recv()
            process(block - core, h)

        @pl.when(serves & (j == steps - 1))
        def _():
            po_src[h] = (acc1[...] / l1[...]).astype(jnp.bfloat16)
            ps_src[h] = (m1[...] + jnp.log2(l1[...])).T[:8, :]
            po_copy(h).start()
            ps_copy(h).start()

        return carry

    advance(jnp.int32(0))
    lax.fori_loop(0, kv_local * steps, attend_step, 0)

    live_all = jnp.concatenate([wide_ref[1]] * HEADS_PER, axis=0) > 0

    def store(h, rows):
        rows = jnp.where(live_all, rows, 0.0).astype(jnp.bfloat16)
        for g in range(HEADS_PER):
            at = pl.multiple_of((h * HEADS_PER + g) * HEAD_DIM, HEAD_DIM)
            out_ref[:, pl.ds(at, HEAD_DIM)] = rows[g * slots : (g + 1) * slots, :]

    def finish(h, carry):
        @pl.when(z < 2)
        def _():
            store(h, acc0[h] / l0[h])

        @pl.when(z >= 2)
        def _():
            po_copy(h).wait_recv()
            ps_copy(h).wait_recv()
            stat = jnp.concatenate([ps_dst[h]] * (HEAD_DIM // 8), axis=0).T
            top = jnp.maximum(m0[h], stat)
            own = jnp.exp2(m0[h] - top)
            far = jnp.exp2(stat - top)
            total = l0[h] * own + far
            store(h, acc0[h] * (own / total) + po_dst[h].astype(jnp.float32) * (far / total))

        return carry

    lax.fori_loop(0, kv_local, finish, 0)

    for k in range(1, n_head):
        drift_copy(k).wait_recv()
    summed = d_buf[0, 0:1, :slots]
    for k in range(1, n_head):
        summed = summed + d_buf[k, 0:1, :slots]
    drift_ref[...] = jnp.where(live_row > 0, summed / (2.0 * KV_HEADS * HEAD_DIM), 0.0)
    for k in range(1, n_head):
        drift_copy(k).wait_send()

    def drain(h, carry):
        each_send(h, lambda c: c.wait_send())

        @pl.when(z >= 2)
        def _():
            q_copy(h).wait_send()

        def drain_block(j, inner):
            block, need = source(j)

            @pl.when(need)
            def _():
                kv_copy(block, h, fw_send.at[j, h], sibling).wait_send()

            return inner

        lax.fori_loop(0, 2 * columns, drain_block, 0)

        @pl.when(serves)
        def _():
            po_copy(h).wait_send()
            ps_copy(h).wait_send()

        return carry

    lax.fori_loop(0, kv_local, drain, 0)


def shards(
    n,
    n_head,
    queries,
    cached_keys,
    cached_values,
    fresh_keys,
    fresh_values,
    recompute_index,
    recompute_count,
    group_offsets,
):
    tokens, width = cached_keys.shape
    slots = queries.shape[0]
    kv_local = width // HEAD_DIM
    own_start = lax.dynamic_index_in_dim(group_offsets, lax.axis_index("ctx"), keepdims=False)
    indices = recompute_index[0]
    live = (jnp.arange(slots, dtype=jnp.int32) < recompute_count[0]).astype(jnp.int32)
    positions = own_start + jnp.concatenate([indices, jnp.zeros((8,), jnp.int32)])
    angles = positions.astype(jnp.float32)[:, None] * inverse_freq()[None, :]
    cosine = jnp.cos(angles)
    sine = jnp.sin(angles)
    cosine = jnp.concatenate([cosine, cosine], axis=1)
    sine = jnp.concatenate([-sine, sine], axis=1)
    meta = jnp.stack([indices, live])
    wide = jnp.broadcast_to(meta[:, :, None], (2, slots, HEAD_DIM))
    rows = slots * HEADS_PER
    half = n // 2
    columns = n // LAYERS // 2
    bf16, f32 = jnp.bfloat16, jnp.float32
    dma = pltpu.SemaphoreType.DMA
    return pl.pallas_call(
        functools.partial(kernel, n, n_head),
        out_shape=(
            jax.ShapeDtypeStruct(queries.shape, bf16),
            jax.ShapeDtypeStruct(cached_keys.shape, bf16),
            jax.ShapeDtypeStruct(cached_values.shape, bf16),
            jax.ShapeDtypeStruct((1, slots), f32),
        ),
        in_specs=[pl.BlockSpec(memory_space=pltpu.VMEM)] * 9,
        out_specs=(pl.BlockSpec(memory_space=pltpu.VMEM),) * 4,
        scratch_shapes=[
            pltpu.VMEM((half, kv_local, 2, tokens, HEAD_DIM), bf16),
            pltpu.VMEM((2, kv_local, rows, HEAD_DIM), bf16),
            pltpu.VMEM((kv_local, rows, HEAD_DIM), f32),
            pltpu.VMEM((kv_local, rows, HEAD_DIM), f32),
            pltpu.VMEM((kv_local, rows, HEAD_DIM), f32),
            pltpu.VMEM((rows, HEAD_DIM), f32),
            pltpu.VMEM((rows, HEAD_DIM), f32),
            pltpu.VMEM((rows, HEAD_DIM), f32),
            pltpu.VMEM((kv_local, rows, HEAD_DIM), bf16),
            pltpu.VMEM((kv_local, 8, rows), f32),
            pltpu.VMEM((kv_local, rows, HEAD_DIM), bf16),
            pltpu.VMEM((kv_local, 8, rows), f32),
            pltpu.VMEM((n_head, 8, HEAD_DIM), f32),
            dma((half, kv_local)),
            dma((2 * columns, kv_local)),
            dma((2 * columns, kv_local)),
            dma((kv_local,)),
            dma((kv_local,)),
            dma((kv_local,)),
            dma((kv_local,)),
            dma((kv_local,)),
            dma((kv_local,)),
            dma((n_head,)),
            dma((n_head,)),
        ],
        compiler_params=pltpu.CompilerParams(
            collective_id=0, has_side_effects=True, vmem_limit_bytes=40 * 1024 * 1024
        ),
        cost_estimate=pl.CostEstimate(
            flops=4 * half * kv_local * tokens * rows * HEAD_DIM,
            bytes_accessed=8 * tokens * width,
            transcendentals=half * kv_local * tokens * rows,
        ),
    )(queries, cached_keys, cached_values, fresh_keys, fresh_values, cosine, sine, meta, wide)


def solution(mesh):
    return jax.shard_map(
        functools.partial(shards, mesh.shape["ctx"], mesh.shape["head"]),
        mesh=mesh,
        in_specs=(
            P("ctx", "head"),
            P("ctx", "head"),
            P("ctx", "head"),
            P("ctx", "head"),
            P("ctx", "head"),
            P("ctx", None),
            P("ctx"),
            P(),
        ),
        out_specs=(P("ctx", "head"), P("ctx", "head"), P("ctx", "head"), P("ctx", None)),
        check_vma=False,
    )
```
